128 devices in a mesh: ka: 4 (over z_hi, core), ga: 32 (over y, z_lo, x).
Axes of the slice: x: 4, y: 4, z: 4 (z_hi: 2, z_lo: 2; z = z_hi * 2 + z_lo), core: 2. Of those that a mesh axis runs over, the one named last changes fastest.
Arguments:
- pair_vc: bfloat16 [384, 2048, 128], P('ka', 'ga'), may hold values from -6 to 6
- coulomb: float32 [2048], P('ga'), may hold values from 0.01 to 0.1
- dens_cc: bfloat16 [2, 384, 2048, 128], P(None, 'ka', 'ga'), may hold values from -1.5 to 1.5
- dens_vv: bfloat16 [2, 384, 2048, 128], P(None, 'ka', 'ga'), may hold values from -1.5 to 1.5
- screen: bfloat16 [2, 2048, 2048], P(None, 'ga'), may hold values from -0.125 to 0.125
- offsets: int32 [2, 2], replicated, may hold values from 0 to 23, as said below
Outputs:
- kernel: float32 [2, 2, 384, 4096], P(None, None, ('ka', 'ga'))
The draws below stay inside these ranges and needn't reach their ends.
Inputs may be any that keep to these rules, and one draw needn't show every extreme that they name: offsets[o, 0] is 1 to 4; one offset, which one drawn from the seed, has offsets[o, 0] = 4 and offsets[o, 1] = 23, the other has offsets[o, 1] = 0.
All inputs are finite; a program needn't handle non-finite values.
Results may differ from the reference program's by a relative error of at most 0.0029.
Values may be sent and summed in bfloat16 or wider, within the bound.
No kernel may reach another device: no remote copies, remote signals or barrier semaphores. Data moves between devices by JAX's collectives and lax.ppermute only.
A program may use at most 192 MiB of HBM per device.

```python
import math
import jax
import jax.numpy as jnp
from jax import lax

NV = 8
NC = 8
NG = 2048
NKY = 24
KX_DEV = 4
NOFF = 2
NKX = 16
NK = 384


def draw_offsets(key, part):
    key = jax.random.fold_in(key, 11)
    first_key, second_key = jax.random.split(key, 2)
    special = jax.random.randint(first_key, (), 0, NOFF)
    row_index = jnp.arange(NOFF)
    steps_x = jax.random.randint(second_key, (NOFF,), 1, KX_DEV + 1)
    steps_x = jnp.where(row_index == special, KX_DEV, steps_x)
    steps_y = jnp.where(row_index == special, NKY - 1, 0)
    return jnp.stack([steps_x, steps_y], axis=1).astype(jnp.int32)


def block_levels(own_key, extent, pieces, low, top_value):
    def one(dim, shards_of):
        heights = jax.random.uniform(jax.random.fold_in(jax.random.fold_in(own_key, 6), dim), (shards_of,), jnp.float32, low / len(pieces), top_value / len(pieces))
        return jnp.repeat(jnp.exp(heights), extent[dim] // shards_of).reshape((-1,) + (1,) * (len(extent) - dim - 1))

    gain = one(*pieces[0])
    for cut in pieces[1:]:
        gain = gain * one(*cut)
    return gain


def bell_draw(own_key, shape, deviation, reach, pieces=(), dtype=jnp.bfloat16):
    array = jax.random.normal(own_key, shape, jnp.float32) * deviation
    if len(pieces) > 0:
        array = block_levels(own_key, shape, pieces, -0.22, 0.18) * array
    return jnp.clip(array, min=-reach, max=reach).astype(dtype)


def setup_inputs(seed: int = 0) -> dict:
    key_of = jax.random.split(jax.random.key(seed), 7)
    pair_vc = bell_draw(key_of[0], (NK, NG, 2 * NV * NC), 1.0, 6.0, ((0, 4), (1, 32)))
    coulomb = jnp.clip(jnp.exp(math.log(0.1) - 2.3025851 * jax.random.uniform(key_of[1], (NG,), jnp.float32) ** block_levels(key_of[1], (NG,), ((0, 32),), -0.2, 0.2)), 0.01, 0.1)
    dens_cc = bell_draw(key_of[2], (NOFF, NK, NG, 2 * NC * NC), 0.25, 1.5, ((1, 4), (2, 32)))
    dens_vv = bell_draw(key_of[3], (NOFF, NK, NG, 2 * NV * NV), 0.25, 1.5, ((1, 4), (2, 32)))
    screen = bell_draw(key_of[4], (NOFF, NG, NG), NG ** -0.5, 0.125, ((1, 32),))
    offsets = draw_offsets(jax.random.fold_in(key_of[6], 71), 0)
    return {"pair_vc": pair_vc, "coulomb": coulomb, "dens_cc": dens_cc, "dens_vv": dens_vv, "screen": screen, "offsets": offsets}


def to_planes(field, width):
    shaped = field.astype(jnp.float32).reshape(NK, NG, 2, width)
    return jnp.transpose(shaped, (2, 0, 3, 1))


def shift_grid(field, step_x, step_y):
    twice = jnp.concatenate([field, field], axis=1)
    field = lax.dynamic_slice_in_dim(twice, step_x, NKX, 1)
    twice = jnp.concatenate([field, field], axis=2)
    return lax.dynamic_slice_in_dim(twice, step_y, NKY, 2)


def pair_products(left_side, right_side):
    real_real = jnp.einsum('kpg,kqg->kpq', left_side[0], right_side[0])
    imag_imag = jnp.einsum('kpg,kqg->kpq', left_side[1], right_side[1])
    real_imag = jnp.einsum('kpg,kqg->kpq', left_side[0], right_side[1])
    imag_real = jnp.einsum('kpg,kqg->kpq', left_side[1], right_side[0])
    return jnp.stack([real_real + imag_imag, real_imag - imag_real])


def reorder_direct(direct):
    shaped = direct.reshape(2, NK, NC, NC, NV, NV)
    shaped = jnp.transpose(shaped, (0, 1, 4, 2, 5, 3))
    return shaped.reshape(2, NK, NV * NC * NV * NC)


def reference(pair_vc, coulomb, dens_cc, dens_vv, screen, offsets):
    pairs = NV * NC
    widened = to_planes(pair_vc, pairs)
    scaled = lax.optimization_barrier((coulomb * widened).astype(jnp.bfloat16)).astype(jnp.float32)
    grid = widened.reshape(2, NKX, NKY, pairs, NG)
    kernels = []
    for offset_index in range(NOFF):
        step_x = offsets[offset_index, 0].astype(jnp.int32)
        step_y = offsets[offset_index, 1].astype(jnp.int32)
        moved = shift_grid(grid, step_x, step_y).reshape(2, NK, pairs, NG)
        exch = pair_products(scaled, moved).reshape(2, NK, pairs * pairs)
        valence = to_planes(dens_vv[offset_index], NV * NV)
        conduction = to_planes(dens_cc[offset_index], NC * NC)
        image = jnp.einsum('gh,ckph->ckpg', screen[offset_index].astype(jnp.float32), valence)
        image = lax.optimization_barrier(image.astype(jnp.bfloat16)).astype(jnp.float32)
        direct = pair_products(conduction, image)
        kernels.append(2.0 * exch - reorder_direct(direct))
    return jnp.stack(kernels)
```

```python
import functools

import jax
import jax.numpy as jnp
from jax import lax
from jax.experimental import pallas as pl
from jax.experimental.pallas import tpu as pltpu
from jax.sharding import PartitionSpec as P

NV = 8
NC = 8
NKY = 24
KX_DEV = 4
NOFF = 2
AXES = ("ka", "ga")
A_STEPS = (0, 0, -1, -1, 1, 1, 2, 2)
Z_STEPS = (0, 1, 0, 1, 0, 1, 0, 1)


def index_of(x, y, z_hi, z_lo, core):
    return (z_hi * 2 + core) * 32 + (y % 4) * 8 + (z_lo % 2) * 4 + x % 4


def route(move):
    pairs = []
    for source in range(128):
        ka, ga = divmod(source, 32)
        z_hi, core = divmod(ka, 2)
        y, rest = divmod(ga, 8)
        z_lo, x = divmod(rest, 4)
        pairs.append((source, move(x, y, z_hi, z_lo, core)))
    return pairs


def along_first(step):
    return route(
        lambda x, y, h, l, c: index_of(x + step, y, h, l, c) if c == 0 else index_of(x, y + step, h, l, c)
    )


def along_second(step):
    return route(
        lambda x, y, h, l, c: index_of(x, y + step, h, l, c) if c == 0 else index_of(x + step, y, h, l, c)
    )


def along_y(step):
    return route(lambda x, y, h, l, c: index_of(x, y + step, h, l, c))


def along_z():
    return route(lambda x, y, h, l, c: index_of(x, y, h, l + 1, c))


def other_core():
    return route(lambda x, y, h, l, c: index_of(x, y, h, l, 1 - c))


def ka_back():
    return [(i, (i - 32) % 128) for i in range(128)]


def ka_back_j_ahead():
    pairs = []
    for source in range(128):
        ka, ga = divmod(source, 32)
        y, j = divmod(ga, 8)
        pairs.append((source, ((ka - 1) % 4) * 32 + y * 8 + (j + 1) % 8))
    return pairs


def send(array, pairs):
    return lax.ppermute(array, AXES, pairs)


def ring_of_four(held, along):
    half = held.shape[0] // 2
    behind = send(held, along(1))
    ahead = send(held, along(-1))
    far_low = send(behind[:half], along(1))
    far_high = send(ahead[half:], along(-1))
    return behind, ahead, far_low, far_high


def direct_kernel(step, first, pos_ref, rows_ref, valence_ref, conduction_ref, sum_ref, out_ref):
    blocks = rows_ref.shape[0]
    x, y, z_lo, core = pos_ref[0], pos_ref[1], pos_ref[2], pos_ref[3]
    along_a = jnp.where(core == 0, x, y)
    along_b = lax.rem(jnp.where(core == 0, y, x) + (step + 4), 4)
    places = []
    for block in range(first, first + blocks):
        a_now = lax.rem(along_a + (A_STEPS[block] + 4), 4)
        z_now = lax.rem(z_lo + Z_STEPS[block], 2)
        x_now = jnp.where(core == 0, a_now, along_b)
        y_now = jnp.where(core == 0, along_b, a_now)
        places.append(y_now * 8 + z_now * 4 + x_now)
    rows = rows_ref[...].reshape(blocks * rows_ref.shape[1], rows_ref.shape[2])
    image = jnp.dot(rows, valence_ref[...], preferred_element_type=jnp.float32).astype(jnp.bfloat16)
    for k in range(conduction_ref.shape[1]):
        left = jnp.concatenate([conduction_ref[place, k] for place in places], axis=0)
        out_ref[k] = sum_ref[k] + lax.dot_general(
            left,
            image[:, k * 128 : (k + 1) * 128],
            (((0,), (0,)), ((), ())),
            preferred_element_type=jnp.float32,
        )


def add_direct(step, first, pos, rows, valence, conduction, total):
    vmem = pl.BlockSpec(memory_space=pltpu.VMEM)
    count = rows.shape[0] * rows.shape[1]
    return pl.pallas_call(
        functools.partial(direct_kernel, step, first),
        out_shape=jax.ShapeDtypeStruct(total.shape, total.dtype),
        in_specs=[pl.BlockSpec(memory_space=pltpu.SMEM), vmem, vmem, vmem, vmem],
        out_specs=vmem,
        input_output_aliases={4: 0},
        compiler_params=pltpu.CompilerParams(vmem_limit_bytes=40 * 1024 * 1024),
        cost_estimate=pl.CostEstimate(
            flops=2 * count * 2048 * 768 + 2 * count * 128 * 768,
            bytes_accessed=8 * 1024 * 1024,
            transcendentals=0,
        ),
    )(pos, rows, valence, conduction, total)


def parts_of(full):
    half = full.shape[-1] // 2
    real_part = full[..., :half, :half] + full[..., half:, half:]
    imag_part = full[..., :half, half:] - full[..., half:, :half]
    return real_part, imag_part


def exchange_sums(pair_vc, coulomb, offsets, y):
    groups = [[b * 8 + i for i in range(8)] for b in range(4)]
    sent = jnp.transpose(pair_vc.reshape(KX_DEV, 8, 3, 64, 128), (1, 0, 2, 3, 4))
    here = lax.all_to_all(
        sent, "ga", split_axis=0, concat_axis=0, tiled=True, axis_index_groups=groups
    )
    all_coulomb = lax.all_gather(coulomb, "ga", axis=0, tiled=True)
    near_coulomb = lax.dynamic_slice_in_dim(all_coulomb, y * 512, 512, 0)
    ahead = send(here, ka_back())
    before = send(here[:, :, 2:], ka_back_j_ahead())
    scaled = (near_coulomb.reshape(8, 1, 1, 64, 1) * here.astype(jnp.float32)).astype(jnp.bfloat16)
    special = jnp.where(offsets[0, 1] == NKY - 1, 0, 1)
    plain_x = offsets[1 - special, 0]
    shifted = jnp.concatenate([before, ahead[:, :, :2]], axis=2)
    joined = jnp.concatenate([here, ahead], axis=1)
    plain = lax.dynamic_slice_in_dim(joined, plain_x, KX_DEV, 1)

    def products(right):
        full = jnp.einsum("sabgp,sabgq->abpq", scaled, right, preferred_element_type=jnp.float32)
        return jnp.stack(parts_of(full), axis=1)

    of_special = products(shifted)
    of_plain = products(plain)
    terms = jnp.stack(
        [jnp.where(special == 0, of_special, of_plain), jnp.where(special == 0, of_plain, of_special)],
        axis=1,
    )
    total = lax.dynamic_index_in_dim(terms, y, 0, keepdims=False)
    for step in (1, 2, 3):
        piece = lax.dynamic_index_in_dim(terms, lax.rem(y + step, 4), 0, keepdims=False)
        total = total + send(piece, along_y(step))
    return total


def own_offset(dens, core):
    mine = lax.dynamic_index_in_dim(dens, core, 0, keepdims=False)
    theirs = lax.dynamic_index_in_dim(dens, 1 - core, 0, keepdims=False)
    got = send(theirs, other_core())
    packed = jnp.concatenate([mine.reshape(32, 3, 64, 128), got.reshape(32, 3, 64, 128)], axis=1)
    return lax.all_to_all(packed, "ga", split_axis=0, concat_axis=0, tiled=True)


def local(pair_vc, coulomb, dens_cc, dens_vv, screen, offsets):
    ka = lax.axis_index("ka")
    ga = lax.axis_index("ga")
    core = lax.rem(ka, 2)
    y, z_lo, x = ga // 8, lax.rem(ga // 4, 2), lax.rem(ga, 4)
    pos = jnp.stack([x, y, z_lo, core]).astype(jnp.int32)

    rows = lax.dynamic_index_in_dim(screen, core, 0, keepdims=True)
    rows = jnp.concatenate([rows, send(rows, along_z())], axis=0)
    rows = jnp.concatenate([rows, *ring_of_four(rows, along_first)], axis=0)
    behind, ahead, far_low, far_high = ring_of_four(rows, along_second)

    valence = own_offset(dens_vv, core)
    conduction = own_offset(dens_cc, core)
    exch = exchange_sums(pair_vc, coulomb, offsets, y)

    valence = jnp.transpose(valence, (0, 2, 1, 3)).reshape(2048, 768)
    total = jnp.zeros((6, 128, 128), jnp.float32)
    total = add_direct(0, 0, pos, rows, valence, conduction, total)
    total = add_direct(-1, 0, pos, behind, valence, conduction, total)
    total = add_direct(1, 0, pos, ahead, valence, conduction, total)
    total = add_direct(2, 0, pos, far_low, valence, conduction, total)
    total = add_direct(2, 4, pos, far_high, valence, conduction, total)

    direct = jnp.stack(parts_of(total))
    mine = direct[:, :3]
    theirs = send(direct[:, 3:], other_core())
    direct = jnp.stack(
        [jnp.where(core == 0, mine, theirs), jnp.where(core == 0, theirs, mine)]
    )
    shaped = direct.reshape(NOFF, 2, 3, NC, NC, NV, NV)
    shaped = jnp.transpose(shaped, (0, 1, 2, 5, 3, 6, 4)).reshape(NOFF, 2, 3, 4096)
    return 2.0 * exch.reshape(NOFF, 2, 3, 4096) - shaped


def solution(mesh):
    placed = (
        P("ka", "ga", None),
        P("ga"),
        P(None, "ka", "ga", None),
        P(None, "ka", "ga", None),
        P(None, "ga", None),
        P(),
    )
    return jax.shard_map(
        local,
        mesh=mesh,
        in_specs=placed,
        out_specs=P(None, None, ("ka", "ga"), None),
        check_vma=False,
    )
```

```python
import functools

import jax
import jax.numpy as jnp
from jax import lax
from jax.experimental import pallas as pl
from jax.experimental.pallas import tpu as pltpu
from jax.sharding import PartitionSpec as P

NV = 8
NC = 8
NKY = 24
KX_DEV = 4
NOFF = 2
AXES = ("ka", "ga")
A_STEPS = (0, 0, -1, -1, 1, 1, 2, 2)
Z_STEPS = (0, 1, 0, 1, 0, 1, 0, 1)


def index_of(x, y, z_hi, z_lo, core):
    return (z_hi * 2 + core) * 32 + (y % 4) * 8 + (z_lo % 2) * 4 + x % 4


def route(move):
    pairs = []
    for source in range(128):
        ka, ga = divmod(source, 32)
        z_hi, core = divmod(ka, 2)
        y, rest = divmod(ga, 8)
        z_lo, x = divmod(rest, 4)
        pairs.append((source, move(x, y, z_hi, z_lo, core)))
    return pairs


def along_first(step):
    return route(
        lambda x, y, h, l, c: index_of(x + step, y, h, l, c) if c == 0 else index_of(x, y + step, h, l, c)
    )


def along_second(step):
    return route(
        lambda x, y, h, l, c: index_of(x, y + step, h, l, c) if c == 0 else index_of(x + step, y, h, l, c)
    )


def along_y(step):
    return route(lambda x, y, h, l, c: index_of(x, y + step, h, l, c))


def along_z():
    return route(lambda x, y, h, l, c: index_of(x, y, h, l + 1, c))


def other_core():
    return route(lambda x, y, h, l, c: index_of(x, y, h, l, 1 - c))


def ka_back():
    return [(i, (i - 32) % 128) for i in range(128)]


def ka_back_j_ahead():
    pairs = []
    for source in range(128):
        ka, ga = divmod(source, 32)
        y, j = divmod(ga, 8)
        pairs.append((source, ((ka - 1) % 4) * 32 + y * 8 + (j + 1) % 8))
    return pairs


def send(array, pairs):
    return lax.ppermute(array, AXES, pairs)


def ring_of_four(held, along):
    half = held.shape[0] // 2
    behind = send(held, along(1))
    ahead = send(held, along(-1))
    far_low = send(behind[:half], along(1))
    far_high = send(ahead[half:], along(-1))
    return behind, ahead, far_low, far_high


def image_kernel(rows_ref, valence_ref, out_ref):
    blocks, depth, width = rows_ref.shape
    rows = rows_ref[...].reshape(blocks * depth, width)
    out_ref[...] = jnp.dot(
        rows, valence_ref[...], preferred_element_type=jnp.float32
    ).astype(jnp.bfloat16)


def image_of(rows, valence):
    vmem = pl.BlockSpec(memory_space=pltpu.VMEM)
    count = rows.shape[0] * rows.shape[1]
    return pl.pallas_call(
        image_kernel,
        out_shape=jax.ShapeDtypeStruct((count, valence.shape[1]), jnp.bfloat16),
        in_specs=[vmem, vmem],
        out_specs=vmem,
        compiler_params=pltpu.CompilerParams(vmem_limit_bytes=40 * 1024 * 1024),
        cost_estimate=pl.CostEstimate(
            flops=2 * count * valence.shape[0] * valence.shape[1],
            bytes_accessed=2 * (count * 2048 + valence.size + count * valence.shape[1]),
            transcendentals=0,
        ),
    )(rows, valence)


def direct_kernel(from_k, pos_ref, own_ref, behind_ref, ahead_ref, low_ref, high_ref, conduction_ref, out_ref):
    x, y, z_lo, core = pos_ref[0], pos_ref[1], pos_ref[2], pos_ref[3]
    along_a = jnp.where(core == 0, x, y)
    along_b = jnp.where(core == 0, y, x)
    places = []
    for step, blocks in ((0, range(8)), (3, range(8)), (1, range(8)), (2, range(8))):
        b_now = lax.rem(along_b + step, 4)
        for block in blocks:
            a_now = lax.rem(along_a + (A_STEPS[block] + 4), 4)
            z_now = lax.rem(z_lo + Z_STEPS[block], 2)
            x_now = jnp.where(core == 0, a_now, b_now)
            y_now = jnp.where(core == 0, b_now, a_now)
            places.append(y_now * 8 + z_now * 4 + x_now)
    lane = lax.broadcasted_iota(jnp.int32, (64, 128), 1)
    for k in range(out_ref.shape[0]):
        columns = pl.ds((from_k + k) * 128, 128)
        full = jnp.zeros((128, 128), jnp.float32)
        first = 0
        for part in (own_ref, behind_ref, ahead_ref, low_ref, high_ref):
            blocks = part.shape[0] // 64
            right = jnp.concatenate(
                [conduction_ref[place, from_k + k] for place in places[first : first + blocks]], axis=0
            )
            first += blocks
            full += lax.dot_general(
                part[:, columns], right, (((0,), (0,)), ((), ())), preferred_element_type=jnp.float32
            )
        turned = pltpu.roll(full[64:], 64, 1)
        out_ref[k] = jnp.where(lane < 64, turned + full[:64], turned - full[:64])


def direct_of(from_k, pos, images, conduction):
    vmem = pl.BlockSpec(memory_space=pltpu.VMEM)
    return pl.pallas_call(
        functools.partial(direct_kernel, from_k),
        out_shape=jax.ShapeDtypeStruct((3, 64, 128), jnp.float32),
        in_specs=[pl.BlockSpec(memory_space=pltpu.SMEM)] + [vmem] * 6,
        out_specs=vmem,
        compiler_params=pltpu.CompilerParams(vmem_limit_bytes=40 * 1024 * 1024),
        cost_estimate=pl.CostEstimate(
            flops=2 * 3 * 2048 * 128 * 128, bytes_accessed=6 * 1024 * 1024, transcendentals=0
        ),
    )(pos, *images, conduction)


def final_kernel(pos_ref, exch_ref, mine_ref, theirs_ref, out_ref, turned_ref):
    core = pos_ref[3]
    lane = lax.broadcasted_iota(jnp.int32, (64, 128), 1)
    row = lax.broadcasted_iota(jnp.int32, (64, 128), 0)
    low_lane = lax.broadcasted_iota(jnp.int32, (32, 128), 1) < 64
    for k in range(3):
        for offset, block in ((core, mine_ref[k]), (1 - core, theirs_ref[k])):
            for step in (1, 2, 4):
                row_bit = (row & step) != 0
                lane_bit = (lane & (8 * step)) != 0
                up = pltpu.roll(pltpu.roll(block, 64 - step, 0), 8 * step, 1)
                down = pltpu.roll(pltpu.roll(block, step, 0), 128 - 8 * step, 1)
                swapped = jnp.where(row_bit, down, up)
                block = jnp.where(row_bit == lane_bit, block, swapped)
            turned_ref[...] = 2.0 * exch_ref[offset, k] - block
            even = turned_ref[pl.ds(0, 32, stride=2), :]
            odd = turned_ref[pl.ds(1, 32, stride=2), :]
            out_ref[offset, k, 0] = jnp.where(low_lane, even, pltpu.roll(odd, 64, 1))
            out_ref[offset, k, 1] = jnp.where(low_lane, pltpu.roll(even, 64, 1), odd)


def finish(pos, exch, mine, theirs):
    vmem = pl.BlockSpec(memory_space=pltpu.VMEM)
    return pl.pallas_call(
        final_kernel,
        out_shape=jax.ShapeDtypeStruct((NOFF, 3, 2, 32, 128), jnp.float32),
        in_specs=[pl.BlockSpec(memory_space=pltpu.SMEM)] + [vmem] * 3,
        out_specs=vmem,
        scratch_shapes=[pltpu.VMEM((64, 128), jnp.float32)],
    )(pos, exch, mine, theirs)


def three_pieces(values):
    high = lax.reduce_precision(values, 8, 7)
    rest = values - high
    middle = lax.reduce_precision(rest, 8, 7)
    low = rest - middle
    return jnp.stack([high, middle, low], axis=-1).astype(jnp.bfloat16)


def exchange_sums(pair_vc, coulomb, offsets, y, wait_for):
    groups = [[b * 8 + i for i in range(8)] for b in range(4)]
    sent = jnp.transpose(pair_vc.reshape(KX_DEV, 8, 3, 64, 128), (1, 0, 2, 3, 4)).reshape(8, 12, 64, 128)
    extra = jnp.pad(three_pieces(coulomb), ((0, 0), (0, 125)))
    sent = jnp.concatenate([sent, jnp.broadcast_to(extra, (8, 1, 64, 128))], axis=1)
    sent, _ = lax.optimization_barrier((sent, wait_for))
    here = lax.all_to_all(
        sent, "ga", split_axis=0, concat_axis=0, tiled=True, axis_index_groups=groups
    )
    near_coulomb = jnp.sum(here[:, 12, :, :3].astype(jnp.float32), axis=-1)
    here = here[:, :12].reshape(8, KX_DEV, 3, 64, 128)
    ahead = send(here, ka_back())
    before = send(here[:, :, 2:], ka_back_j_ahead())
    scaled = (near_coulomb.reshape(8, 1, 1, 64, 1) * here.astype(jnp.float32)).astype(jnp.bfloat16)
    special = jnp.where(offsets[0, 1] == NKY - 1, 0, 1)
    plain_x = offsets[1 - special, 0]
    shifted = jnp.concatenate([before, ahead[:, :, :2]], axis=2)
    joined = jnp.concatenate([here, ahead], axis=1)
    plain = lax.dynamic_slice_in_dim(joined, plain_x, KX_DEV, 1)

    def products(right):
        full = jnp.einsum("sabgp,sabgq->abpq", scaled, right, preferred_element_type=jnp.float32)
        half = full.shape[-1] // 2
        real_part = full[..., :half, :half] + full[..., half:, half:]
        imag_part = full[..., :half, half:] - full[..., half:, :half]
        return jnp.concatenate([real_part, imag_part], axis=-1)

    of_special = products(shifted)
    of_plain = products(plain)
    terms = jnp.stack(
        [jnp.where(special == 0, of_special, of_plain), jnp.where(special == 0, of_plain, of_special)],
        axis=1,
    )
    total = lax.dynamic_index_in_dim(terms, y, 0, keepdims=False)
    for step in (1, 2, 3):
        piece = lax.dynamic_index_in_dim(terms, lax.rem(y + step, 4), 0, keepdims=False)
        total = total + send(piece, along_y(step))
    return total


def swapped(dens, core):
    mine = lax.dynamic_index_in_dim(dens, core, 0, keepdims=False)
    theirs = lax.dynamic_index_in_dim(dens, 1 - core, 0, keepdims=False)
    got = send(theirs, other_core())
    return jnp.concatenate([mine.reshape(32, 3, 64, 128), got.reshape(32, 3, 64, 128)], axis=1)


def spread(packed):
    return lax.all_to_all(packed, "ga", split_axis=0, concat_axis=0, tiled=True)


def local(pair_vc, coulomb, dens_cc, dens_vv, screen, offsets):
    ka = lax.axis_index("ka")
    ga = lax.axis_index("ga")
    core = lax.rem(ka, 2)
    y, z_lo, x = ga // 8, lax.rem(ga // 4, 2), lax.rem(ga, 4)
    pos = jnp.stack([x, y, z_lo, core]).astype(jnp.int32)

    rows = lax.dynamic_index_in_dim(screen, core, 0, keepdims=True)
    rows = jnp.concatenate([rows, send(rows, along_z())], axis=0)
    exch = exchange_sums(pair_vc, coulomb, offsets, y, rows)
    rows = jnp.concatenate([rows, *ring_of_four(rows, along_first)], axis=0)
    valence = swapped(dens_vv, core)
    conduction = swapped(dens_cc, core)
    valence, rows = lax.optimization_barrier((valence, rows))
    behind, ahead, far_low, far_high = ring_of_four(rows, along_second)
    valence = spread(valence)
    conduction, _ = lax.optimization_barrier((conduction, valence))
    conduction = spread(conduction)

    valence = jnp.transpose(valence, (0, 2, 1, 3)).reshape(2048, 768)
    images = [image_of(part, valence) for part in (rows, behind, ahead, far_low, far_high)]
    theirs = send(direct_of(3, pos, images, conduction), other_core())
    mine = direct_of(0, pos, images, conduction)
    out = finish(pos, exch, mine, theirs)
    return jnp.transpose(out, (0, 2, 1, 3, 4)).reshape(NOFF, 2, 3, 4096)


def solution(mesh):
    placed = (
        P("ka", "ga", None),
        P("ga"),
        P(None, "ka", "ga", None),
        P(None, "ka", "ga", None),
        P(None, "ga", None),
        P(),
    )
    return jax.shard_map(
        local,
        mesh=mesh,
        in_specs=placed,
        out_specs=P(None, None, ("ka", "ga"), None),
        check_vma=False,
    )
```

```python
import functools

import jax
import jax.numpy as jnp
from jax import lax
from jax.experimental import pallas as pl
from jax.experimental.pallas import tpu as pltpu
from jax.sharding import PartitionSpec as P

NV = 8
NC = 8
NKY = 24
KX_DEV = 4
NOFF = 2
AXES = ("ka", "ga")
A_STEPS = (0, 0, -1, -1, 1, 1, 2, 2)
Z_STEPS = (0, 1, 0, 1, 0, 1, 0, 1)
B_STEPS = (0, -1, 1, 2)


def index_of(x, y, z_hi, z_lo, core):
    return (z_hi * 2 + core) * 32 + (y % 4) * 8 + (z_lo % 2) * 4 + x % 4


def route(move):
    pairs = []
    for source in range(128):
        ka, ga = divmod(source, 32)
        z_hi, core = divmod(ka, 2)
        y, rest = divmod(ga, 8)
        z_lo, x = divmod(rest, 4)
        pairs.append((source, move(x, y, z_hi, z_lo, core)))
    return pairs


def along_first(step):
    return route(
        lambda x, y, h, l, c: index_of(x + step, y, h, l, c) if c == 0 else index_of(x, y + step, h, l, c)
    )


def along_second(step):
    return route(
        lambda x, y, h, l, c: index_of(x, y + step, h, l, c) if c == 0 else index_of(x + step, y, h, l, c)
    )


def along_y(step):
    return route(lambda x, y, h, l, c: index_of(x, y + step, h, l, c))


def along_z():
    return route(lambda x, y, h, l, c: index_of(x, y, h, l + 1, c))


def other_core():
    return route(lambda x, y, h, l, c: index_of(x, y, h, l, 1 - c))


def ka_back():
    return [(i, (i - 32) % 128) for i in range(128)]


def ka_back_j_ahead():
    pairs = []
    for source in range(128):
        ka, ga = divmod(source, 32)
        y, j = divmod(ga, 8)
        pairs.append((source, ((ka - 1) % 4) * 32 + y * 8 + (j + 1) % 8))
    return pairs


def send(array, pairs):
    return lax.ppermute(array, AXES, pairs)


def image_kernel(*refs):
    valence_ref, out_ref = refs[-2], refs[-1]
    first = 0
    for rows_ref in refs[:-2]:
        blocks, depth, width = rows_ref.shape
        for block in range(0, blocks, 4):
            rows = rows_ref[block : block + 4].reshape(4 * depth, width)
            out_ref[first : first + 4 * depth] = jnp.dot(
                rows, valence_ref[...], preferred_element_type=jnp.float32
            ).astype(jnp.bfloat16)
            first += 4 * depth


def image_of(parts, valence):
    vmem = pl.BlockSpec(memory_space=pltpu.VMEM)
    count = sum(part.shape[0] * part.shape[1] for part in parts)
    return pl.pallas_call(
        image_kernel,
        out_shape=jax.ShapeDtypeStruct((count, valence.shape[1]), jnp.bfloat16),
        in_specs=[vmem] * (len(parts) + 1),
        out_specs=vmem,
        compiler_params=pltpu.CompilerParams(vmem_limit_bytes=28 * 1024 * 1024),
        cost_estimate=pl.CostEstimate(
            flops=2 * count * valence.shape[0] * valence.shape[1],
            bytes_accessed=2 * (count * 2048 + valence.size + count * valence.shape[1]),
            transcendentals=0,
        ),
    )(*parts, valence)


def direct_kernel(from_k, pos_ref, *refs):
    parts, conduction_ref, out_ref = refs[:-2], refs[-2], refs[-1]
    x, y, z_lo, core = pos_ref[0], pos_ref[1], pos_ref[2], pos_ref[3]
    along_a = jnp.where(core == 0, x, y)
    along_b = jnp.where(core == 0, y, x)
    places = []
    for step in B_STEPS:
        b_now = lax.rem(along_b + (step + 4), 4)
        for block in range(8):
            a_now = lax.rem(along_a + (A_STEPS[block] + 4), 4)
            z_now = lax.rem(z_lo + Z_STEPS[block], 2)
            x_now = jnp.where(core == 0, a_now, b_now)
            y_now = jnp.where(core == 0, b_now, a_now)
            places.append(y_now * 8 + z_now * 4 + x_now)
    lane = lax.broadcasted_iota(jnp.int32, (64, 128), 1)
    for k in range(out_ref.shape[0]):
        columns = pl.ds((from_k + k) * 128, 128)
        full = jnp.zeros((128, 128), jnp.float32)
        first = 0
        for part in parts:
            blocks = part.shape[0] // 64
            right = jnp.concatenate(
                [conduction_ref[place, from_k + k] for place in places[first : first + blocks]], axis=0
            )
            first += blocks
            full += lax.dot_general(
                part[:, columns], right, (((0,), (0,)), ((), ())), preferred_element_type=jnp.float32
            )
        turned = pltpu.roll(full[64:], 64, 1)
        out_ref[k] = jnp.where(lane < 64, turned + full[:64], turned - full[:64])


def direct_of(from_k, pos, images, conduction):
    vmem = pl.BlockSpec(memory_space=pltpu.VMEM)
    return pl.pallas_call(
        functools.partial(direct_kernel, from_k),
        out_shape=jax.ShapeDtypeStruct((3, 64, 128), jnp.float32),
        in_specs=[pl.BlockSpec(memory_space=pltpu.SMEM)] + [vmem] * (len(images) + 1),
        out_specs=vmem,
        compiler_params=pltpu.CompilerParams(vmem_limit_bytes=20 * 1024 * 1024),
        cost_estimate=pl.CostEstimate(
            flops=2 * 3 * 2048 * 128 * 128, bytes_accessed=6 * 1024 * 1024, transcendentals=0
        ),
    )(pos, *images, conduction)


def final_kernel(pos_ref, exch_0, exch_1, exch_2, exch_3, mine_ref, theirs_ref, out_ref):
    core = pos_ref[3]
    lane = lax.broadcasted_iota(jnp.int32, (64, 128), 1)
    row = lax.broadcasted_iota(jnp.int32, (64, 128), 0)

    def exchanged(block, row_step, lane_step):
        row_bit = (row & row_step) != 0
        lane_bit = (lane & lane_step) != 0
        up = pltpu.roll(pltpu.roll(block, 64 - row_step, 0), lane_step, 1)
        down = pltpu.roll(pltpu.roll(block, row_step, 0), 128 - lane_step, 1)
        return jnp.where(row_bit == lane_bit, block, jnp.where(row_bit, down, up))

    for k in range(3):
        for offset, block in ((core, mine_ref[k]), (1 - core, theirs_ref[k])):
            for step in (1, 2, 4):
                block = exchanged(block, step, 8 * step)
            exch = (exch_0[offset, k] + exch_1[offset, k]) + (exch_2[offset, k] + exch_3[offset, k])
            out_ref[offset, k] = exchanged(2.0 * exch - block, 1, 64)


def finish(pos, exch, mine, theirs):
    vmem = pl.BlockSpec(memory_space=pltpu.VMEM)
    return pl.pallas_call(
        final_kernel,
        out_shape=jax.ShapeDtypeStruct((NOFF, 3, 64, 128), jnp.float32),
        in_specs=[pl.BlockSpec(memory_space=pltpu.SMEM)] + [vmem] * 6,
        out_specs=vmem,
    )(pos, *exch, mine, theirs)


def three_pieces(values):
    high = lax.reduce_precision(values, 8, 7)
    rest = values - high
    middle = lax.reduce_precision(rest, 8, 7)
    low = rest - middle
    return jnp.stack([high, middle, low], axis=-1).astype(jnp.bfloat16)


def exchange_spread(pair_vc, coulomb):
    main = pair_vc.reshape(KX_DEV, 8, 3, 64, 128)
    last = main[:, :, 2:]
    before = jnp.concatenate([last[:, 7:], last[:, :7]], axis=1)
    sent = jnp.concatenate([before, main], axis=2)
    sent = jnp.transpose(sent, (1, 0, 2, 3, 4)).reshape(8, 16, 64, 128)
    extra = jnp.pad(three_pieces(coulomb), ((0, 0), (0, 125)))
    return jnp.concatenate([sent, jnp.broadcast_to(extra, (8, 1, 64, 128))], axis=1)


def exchange_sums(here, ahead, near_coulomb, offsets, y):
    left = here[:, :, 1:].astype(jnp.float32)
    scaled = (near_coulomb.reshape(8, 1, 1, 64, 1) * left).astype(jnp.bfloat16)
    special = jnp.where(offsets[0, 1] == NKY - 1, 0, 1)
    plain_x = offsets[1 - special, 0]
    shifted = ahead[:, :, :3]
    joined = jnp.concatenate([here[:, :, 1:], ahead[:, :, 1:]], axis=1)
    plain = lax.dynamic_slice_in_dim(joined, plain_x, KX_DEV, 1)

    def products(right):
        full = jnp.einsum("sabgp,sabgq->abpq", scaled, right, preferred_element_type=jnp.float32)
        half = full.shape[-1] // 2
        real_part = full[..., :half, :half] + full[..., half:, half:]
        imag_part = full[..., :half, half:] - full[..., half:, :half]
        return jnp.concatenate([real_part, imag_part], axis=-1)

    of_special = products(shifted)
    of_plain = products(plain)
    terms = jnp.stack(
        [jnp.where(special == 0, of_special, of_plain), jnp.where(special == 0, of_plain, of_special)],
        axis=1,
    )
    pieces = [lax.dynamic_index_in_dim(terms, y, 0, keepdims=False)]
    for step in (1, 2, 3):
        piece = lax.dynamic_index_in_dim(terms, lax.rem(y + step, 4), 0, keepdims=False)
        pieces.append(send(piece, along_y(step)))
    return pieces


def both_cores(dens, core):
    mine = lax.dynamic_index_in_dim(dens, core, 0, keepdims=False)
    theirs = lax.dynamic_index_in_dim(dens, 1 - core, 0, keepdims=False)
    got = send(theirs, other_core())
    return jnp.concatenate([mine.reshape(32, 3, 64, 128), got.reshape(32, 3, 64, 128)], axis=1)


def spread(packed, groups=None):
    return lax.all_to_all(
        packed, "ga", split_axis=0, concat_axis=0, tiled=True, axis_index_groups=groups
    )


def local(pair_vc, coulomb, dens_cc, dens_vv, screen, offsets):
    ka = lax.axis_index("ka")
    ga = lax.axis_index("ga")
    core = lax.rem(ka, 2)
    y, z_lo, x = ga // 8, lax.rem(ga // 4, 2), lax.rem(ga, 4)
    pos = jnp.stack([x, y, z_lo, core]).astype(jnp.int32)
    after = lax.optimization_barrier

    rows = lax.dynamic_index_in_dim(screen, core, 0, keepdims=True)
    rows = jnp.concatenate([rows, send(rows, along_z())], axis=0)
    sent = exchange_spread(pair_vc, coulomb)
    sent, rows = after((sent, rows))
    near = [send(rows, along_first(step)) for step in (1, -1)]
    across = send(rows, along_first(2))
    here = spread(sent, [[b * 8 + i for i in range(8)] for b in range(4)])
    valence = both_cores(dens_vv, core)
    valence, near, across = after((valence, near, across))
    rows = jnp.concatenate([rows, *near, across], axis=0)
    behind = send(rows, along_second(1))
    ahead = send(rows, along_second(-1))
    valence = spread(valence)

    near_coulomb = jnp.sum(here[:, 16, :, :3].astype(jnp.float32), axis=-1)
    here = here[:, :16].reshape(8, KX_DEV, 4, 64, 128)
    next_rows = send(here, ka_back())

    conduction = both_cores(dens_cc, core)
    conduction, valence, next_rows, behind, ahead = after((conduction, valence, next_rows, behind, ahead))
    far_low, far_high = send(behind[:4], along_second(1)), send(ahead[4:], along_second(-1))
    conduction = spread(conduction)

    valence = jnp.transpose(valence, (0, 2, 1, 3)).reshape(2048, 768)
    images = [image_of((rows, behind, ahead), valence), image_of((far_low, far_high), valence)]
    exch = exchange_sums(here, next_rows, near_coulomb, offsets, y)

    theirs = send(direct_of(3, pos, images, conduction), other_core())
    mine = direct_of(0, pos, images, conduction)
    out = finish(pos, exch, mine, theirs).reshape(NOFF, 3, 32, 2, 128)
    return jnp.transpose(out, (0, 3, 1, 2, 4)).reshape(NOFF, 2, 3, 4096)


def solution(mesh):
    placed = (
        P("ka", "ga", None),
        P("ga"),
        P(None, "ka", "ga", None),
        P(None, "ka", "ga", None),
        P(None, "ga", None),
        P(),
    )
    return jax.shard_map(
        local,
        mesh=mesh,
        in_specs=placed,
        out_specs=P(None, None, ("ka", "ga"), None),
        check_vma=False,
    )
```

```python
import functools

import jax
import jax.numpy as jnp
from jax import lax
from jax.experimental import pallas as pl
from jax.experimental.pallas import tpu as pltpu
from jax.sharding import PartitionSpec as P

NV = 8
NC = 8
NKY = 24
KX_DEV = 4
NOFF = 2
AXES = ("ka", "ga")
A_STEPS = (0, 0, -1, -1, 1, 1, 2, 2)
Z_STEPS = (0, 1, 0, 1, 0, 1, 0, 1)
B_STEPS = (0, -1, 1, 2)


def index_of(x, y, z_hi, z_lo, core):
    return (z_hi * 2 + core) * 32 + (y % 4) * 8 + (z_lo % 2) * 4 + x % 4


def route(move):
    pairs = []
    for source in range(128):
        ka, ga = divmod(source, 32)
        z_hi, core = divmod(ka, 2)
        y, rest = divmod(ga, 8)
        z_lo, x = divmod(rest, 4)
        pairs.append((source, move(x, y, z_hi, z_lo, core)))
    return pairs


def along_first(step):
    return route(
        lambda x, y, h, l, c: index_of(x + step, y, h, l, c) if c == 0 else index_of(x, y + step, h, l, c)
    )


def along_second(step):
    return route(
        lambda x, y, h, l, c: index_of(x, y + step, h, l, c) if c == 0 else index_of(x + step, y, h, l, c)
    )


def along_y(step):
    return route(lambda x, y, h, l, c: index_of(x, y + step, h, l, c))


def along_z():
    return route(lambda x, y, h, l, c: index_of(x, y, h, l + 1, c))


def other_core():
    return route(lambda x, y, h, l, c: index_of(x, y, h, l, 1 - c))


def ka_back():
    return [(i, (i - 32) % 128) for i in range(128)]


def ka_back_j_ahead():
    pairs = []
    for source in range(128):
        ka, ga = divmod(source, 32)
        y, j = divmod(ga, 8)
        pairs.append((source, ((ka - 1) % 4) * 32 + y * 8 + (j + 1) % 8))
    return pairs


def send(array, pairs):
    return lax.ppermute(array, AXES, pairs)


def image_kernel(*refs):
    valence_ref, out_ref = refs[-2], refs[-1]
    first = 0
    for rows_ref in refs[:-2]:
        blocks, depth, width = rows_ref.shape
        for block in range(0, blocks, 4):
            rows = rows_ref[block : block + 4].reshape(4 * depth, width)
            image = jnp.dot(rows, valence_ref[...], preferred_element_type=jnp.float32).astype(jnp.bfloat16)
            for k in range(6):
                out_ref[k, first : first + 4 * depth] = image[:, k * 128 : (k + 1) * 128]
            first += 4 * depth


def image_of(parts, valence):
    vmem = pl.BlockSpec(memory_space=pltpu.VMEM)
    count = sum(part.shape[0] * part.shape[1] for part in parts)
    return pl.pallas_call(
        image_kernel,
        out_shape=jax.ShapeDtypeStruct((6, count, 128), jnp.bfloat16),
        in_specs=[vmem] * (len(parts) + 1),
        out_specs=vmem,
        compiler_params=pltpu.CompilerParams(vmem_limit_bytes=18 * 1024 * 1024),
        cost_estimate=pl.CostEstimate(
            flops=2 * count * valence.shape[0] * valence.shape[1],
            bytes_accessed=2 * (count * 2048 + valence.size + count * valence.shape[1]),
            transcendentals=0,
        ),
    )(*parts, valence)


def traded(block, row_step, lane_step):
    row_bit = (lax.broadcasted_iota(jnp.int32, (64, 128), 0) & row_step) != 0
    lane_bit = (lax.broadcasted_iota(jnp.int32, (64, 128), 1) & lane_step) != 0
    up = pltpu.roll(pltpu.roll(block, 64 - row_step, 0), lane_step, 1)
    down = pltpu.roll(pltpu.roll(block, row_step, 0), 128 - lane_step, 1)
    return jnp.where(row_bit == lane_bit, block, jnp.where(row_bit, down, up))


def direct_kernel(pos_ref, near_ref, far_ref, conduction_ref, theirs_ref, mine_ref, image, right, sems):
    x, y, z_lo, core = pos_ref[0], pos_ref[1], pos_ref[2], pos_ref[3]
    along_a = jnp.where(core == 0, x, y)
    along_b = jnp.where(core == 0, y, x)
    split = near_ref.shape[1]
    order = (3, 4, 5, 0, 1, 2)

    def copies(k):
        return (
            pltpu.make_async_copy(near_ref.at[k], image.at[k, pl.ds(0, split)], sems.at[k, 0]),
            pltpu.make_async_copy(far_ref.at[k], image.at[k, pl.ds(split, 2048 - split)], sems.at[k, 1]),
            pltpu.make_async_copy(conduction_ref.at[:, k], right.at[k], sems.at[k, 2]),
        )

    for k in order:
        for copy in copies(k):
            copy.start()
    places = []
    for step in B_STEPS:
        b_now = lax.rem(along_b + (step + 4), 4)
        for block in range(8):
            a_now = lax.rem(along_a + (A_STEPS[block] + 4), 4)
            z_now = lax.rem(z_lo + Z_STEPS[block], 2)
            x_now = jnp.where(core == 0, a_now, b_now)
            y_now = jnp.where(core == 0, b_now, a_now)
            places.append(y_now * 8 + z_now * 4 + x_now)
    lane = lax.broadcasted_iota(jnp.int32, (64, 128), 1)
    for k in order:
        for copy in copies(k):
            copy.wait()
        gathered = jnp.concatenate([right[k, place] for place in places], axis=0)
        full = lax.dot_general(
            image[k], gathered, (((0,), (0,)), ((), ())), preferred_element_type=jnp.float32
        )
        turned = pltpu.roll(full[64:], 64, 1)
        block = jnp.where(lane < 64, turned + full[:64], turned - full[:64])
        for row_step, lane_step in ((1, 8), (2, 16), (4, 32), (1, 64)):
            block = traded(block, row_step, lane_step)
        if k < 3:
            mine_ref[k] = block
        else:
            theirs_ref[k - 3] = block


def direct_of(pos, images, conduction):
    vmem = pl.BlockSpec(memory_space=pltpu.VMEM)
    shape = jax.ShapeDtypeStruct((3, 64, 128), jnp.float32)
    return pl.pallas_call(
        direct_kernel,
        out_shape=(shape, shape),
        in_specs=[pl.BlockSpec(memory_space=pltpu.SMEM)] + [pl.BlockSpec(memory_space=pl.ANY)] * 3,
        out_specs=(vmem, vmem),
        scratch_shapes=[
            pltpu.VMEM((6, 2048, 128), jnp.bfloat16),
            pltpu.VMEM((6, 32, 64, 128), jnp.bfloat16),
            pltpu.SemaphoreType.DMA((6, 3)),
        ],
        compiler_params=pltpu.CompilerParams(vmem_limit_bytes=60 * 1024 * 1024),
        cost_estimate=pl.CostEstimate(
            flops=2 * 6 * 2048 * 128 * 128, bytes_accessed=7 * 1024 * 1024, transcendentals=0
        ),
    )(pos, *images, conduction)


def exchange_kernel(first_ref, second_ref, third_ref, fourth_ref, out_ref):
    for offset in range(NOFF):
        for k in range(3):
            total = (first_ref[offset, k] + second_ref[offset, k]) + (
                third_ref[offset, k] + fourth_ref[offset, k]
            )
            out_ref[offset, k] = traded(2.0 * total, 1, 64)


def exchange_of(pieces):
    vmem = pl.BlockSpec(memory_space=pltpu.VMEM)
    return pl.pallas_call(
        exchange_kernel,
        out_shape=jax.ShapeDtypeStruct((NOFF, 3, 64, 128), jnp.float32),
        in_specs=[vmem] * 4,
        out_specs=vmem,
    )(*pieces)


def three_pieces(values):
    high = lax.reduce_precision(values, 8, 7)
    rest = values - high
    middle = lax.reduce_precision(rest, 8, 7)
    low = rest - middle
    return jnp.stack([high, middle, low], axis=-1).astype(jnp.bfloat16)


def exchange_spread(pair_vc, coulomb):
    main = pair_vc.reshape(KX_DEV, 8, 3, 64, 128)
    last = main[:, :, 2:]
    before = jnp.concatenate([last[:, 7:], last[:, :7]], axis=1)
    sent = jnp.concatenate([before, main], axis=2)
    sent = jnp.transpose(sent, (1, 0, 2, 3, 4)).reshape(8, 16, 64, 128)
    extra = jnp.pad(three_pieces(coulomb), ((0, 0), (0, 125)))
    return jnp.concatenate([sent, jnp.broadcast_to(extra, (8, 1, 64, 128))], axis=1)


def exchange_sums(here, ahead, near_coulomb, offsets, y):
    left = here[:, :, 1:].astype(jnp.float32)
    scaled = (near_coulomb.reshape(8, 1, 1, 64, 1) * left).astype(jnp.bfloat16)
    special = jnp.where(offsets[0, 1] == NKY - 1, 0, 1)
    plain_x = offsets[1 - special, 0]
    shifted = ahead[:, :, :3]
    joined = jnp.concatenate([here[:, :, 1:], ahead[:, :, 1:]], axis=1)
    plain = lax.dynamic_slice_in_dim(joined, plain_x, KX_DEV, 1)

    def products(right):
        full = jnp.einsum("sabgp,sabgq->abpq", scaled, right, preferred_element_type=jnp.float32)
        half = full.shape[-1] // 2
        real_part = full[..., :half, :half] + full[..., half:, half:]
        imag_part = full[..., :half, half:] - full[..., half:, :half]
        return jnp.concatenate([real_part, imag_part], axis=-1)

    of_special = products(shifted)
    of_plain = products(plain)
    terms = jnp.stack(
        [jnp.where(special == 0, of_special, of_plain), jnp.where(special == 0, of_plain, of_special)],
        axis=1,
    )
    pieces = [lax.dynamic_index_in_dim(terms, y, 0, keepdims=False)]
    for step in (1, 2, 3):
        piece = lax.dynamic_index_in_dim(terms, lax.rem(y + step, 4), 0, keepdims=False)
        pieces.append(send(piece, along_y(step)))
    return pieces


def both_cores(dens, core):
    mine = lax.dynamic_index_in_dim(dens, core, 0, keepdims=False)
    theirs = lax.dynamic_index_in_dim(dens, 1 - core, 0, keepdims=False)
    got = send(theirs, other_core())
    return jnp.concatenate([mine.reshape(32, 3, 64, 128), got.reshape(32, 3, 64, 128)], axis=1)


def spread(packed, groups=None):
    return lax.all_to_all(
        packed, "ga", split_axis=0, concat_axis=0, tiled=True, axis_index_groups=groups
    )


def local(pair_vc, coulomb, dens_cc, dens_vv, screen, offsets):
    ka = lax.axis_index("ka")
    ga = lax.axis_index("ga")
    core = lax.rem(ka, 2)
    y, z_lo, x = ga // 8, lax.rem(ga // 4, 2), lax.rem(ga, 4)
    pos = jnp.stack([x, y, z_lo, core]).astype(jnp.int32)
    after = lax.optimization_barrier

    rows = lax.dynamic_index_in_dim(screen, core, 0, keepdims=True)
    rows = jnp.concatenate([rows, send(rows, along_z())], axis=0)
    sent = exchange_spread(pair_vc, coulomb)
    sent, rows = after((sent, rows))
    near = [send(rows, along_first(step)) for step in (1, -1)]
    across = send(rows, along_first(2))
    here = spread(sent, [[b * 8 + i for i in range(8)] for b in range(4)])
    valence = both_cores(dens_vv, core)
    valence, near, across = after((valence, near, across))
    rows = jnp.concatenate([rows, *near, across], axis=0)
    behind = send(rows, along_second(1))
    ahead = send(rows, along_second(-1))
    valence = spread(valence)

    near_coulomb = jnp.sum(here[:, 16, :, :3].astype(jnp.float32), axis=-1)
    here = here[:, :16].reshape(8, KX_DEV, 4, 64, 128)
    next_rows = send(here, ka_back())

    conduction = both_cores(dens_cc, core)
    conduction, valence, next_rows, behind, ahead = after((conduction, valence, next_rows, behind, ahead))
    far_low, far_high = send(behind[:4], along_second(1)), send(ahead[4:], along_second(-1))
    conduction = spread(conduction)

    valence = jnp.transpose(valence, (0, 2, 1, 3)).reshape(2048, 768)
    images = [image_of((rows, behind, ahead), valence), image_of((far_low, far_high), valence)]
    exch = exchange_sums(here, next_rows, near_coulomb, offsets, y)

    theirs, mine = direct_of(pos, images, conduction)
    theirs = send(theirs, other_core())
    direct = jnp.where((jnp.arange(NOFF) == core)[:, None, None, None], mine[None], theirs[None])
    out = (exchange_of(exch) - direct).reshape(NOFF, 3, 32, 2, 128)
    return jnp.transpose(out, (0, 3, 1, 2, 4)).reshape(NOFF, 2, 3, 4096)


def solution(mesh):
    placed = (
        P("ka", "ga", None),
        P("ga"),
        P(None, "ka", "ga", None),
        P(None, "ka", "ga", None),
        P(None, "ga", None),
        P(),
    )
    return jax.shard_map(
        local,
        mesh=mesh,
        in_specs=placed,
        out_specs=P(None, None, ("ka", "ga"), None),
        check_vma=False,
    )
```

```python
import functools

import jax
import jax.numpy as jnp
from jax import lax
from jax.experimental import pallas as pl
from jax.experimental.pallas import tpu as pltpu
from jax.sharding import PartitionSpec as P

NV = 8
NC = 8
NKY = 24
KX_DEV = 4
NOFF = 2
AXES = ("ka", "ga")
A_STEPS = (0, 0, -1, -1, 1, 1, 2, 2)
Z_STEPS = (0, 1, 0, 1, 0, 1, 0, 1)
B_STEPS = (0, -1, 1, 2)


def index_of(x, y, z_hi, z_lo, core):
    return (z_hi * 2 + core) * 32 + (y % 4) * 8 + (z_lo % 2) * 4 + x % 4


def route(move):
    pairs = []
    for source in range(128):
        ka, ga = divmod(source, 32)
        z_hi, core = divmod(ka, 2)
        y, rest = divmod(ga, 8)
        z_lo, x = divmod(rest, 4)
        pairs.append((source, move(x, y, z_hi, z_lo, core)))
    return pairs


def along_first(step):
    return route(
        lambda x, y, h, l, c: index_of(x + step, y, h, l, c) if c == 0 else index_of(x, y + step, h, l, c)
    )


def along_second(step):
    return route(
        lambda x, y, h, l, c: index_of(x, y + step, h, l, c) if c == 0 else index_of(x + step, y, h, l, c)
    )


def along_y(step):
    return route(lambda x, y, h, l, c: index_of(x, y + step, h, l, c))


def along_z():
    return route(lambda x, y, h, l, c: index_of(x, y, h, l + 1, c))


def other_core():
    return route(lambda x, y, h, l, c: index_of(x, y, h, l, 1 - c))


def ka_back():
    return [(i, (i - 32) % 128) for i in range(128)]


def ka_back_j_ahead():
    pairs = []
    for source in range(128):
        ka, ga = divmod(source, 32)
        y, j = divmod(ga, 8)
        pairs.append((source, ((ka - 1) % 4) * 32 + y * 8 + (j + 1) % 8))
    return pairs


def send(array, pairs):
    return lax.ppermute(array, AXES, pairs)


def image_kernel(*refs):
    valence_ref, out_ref = refs[-2], refs[-1]
    first = 0
    for rows_ref in refs[:-2]:
        blocks, depth, width = rows_ref.shape
        for block in range(0, blocks, 4):
            rows = rows_ref[block : block + 4].reshape(4 * depth, width)
            image = jnp.dot(rows, valence_ref[...], preferred_element_type=jnp.float32).astype(jnp.bfloat16)
            for k in range(6):
                out_ref[k, first : first + 4 * depth] = image[:, k * 128 : (k + 1) * 128]
            first += 4 * depth


def image_of(parts, valence):
    vmem = pl.BlockSpec(memory_space=pltpu.VMEM)
    count = sum(part.shape[0] * part.shape[1] for part in parts)
    return pl.pallas_call(
        image_kernel,
        out_shape=jax.ShapeDtypeStruct((6, count, 128), jnp.bfloat16),
        in_specs=[vmem] * (len(parts) + 1),
        out_specs=vmem,
        compiler_params=pltpu.CompilerParams(vmem_limit_bytes=18 * 1024 * 1024),
        cost_estimate=pl.CostEstimate(
            flops=2 * count * valence.shape[0] * valence.shape[1],
            bytes_accessed=2 * (count * 2048 + valence.size + count * valence.shape[1]),
            transcendentals=0,
        ),
    )(*parts, valence)


def traded(block, row_step, lane_step):
    row_bit = (lax.broadcasted_iota(jnp.int32, (64, 128), 0) & row_step) != 0
    lane_bit = (lax.broadcasted_iota(jnp.int32, (64, 128), 1) & lane_step) != 0
    up = pltpu.roll(pltpu.roll(block, 64 - row_step, 0), lane_step, 1)
    down = pltpu.roll(pltpu.roll(block, row_step, 0), 128 - lane_step, 1)
    return jnp.where(row_bit == lane_bit, block, jnp.where(row_bit, down, up))


def direct_kernel(pos_ref, near_ref, far_ref, conduction_ref, theirs_ref, mine_ref, image, right, sems):
    x, y, z_lo, core = pos_ref[0], pos_ref[1], pos_ref[2], pos_ref[3]
    along_a = jnp.where(core == 0, x, y)
    along_b = jnp.where(core == 0, y, x)
    split = near_ref.shape[1]
    order = (3, 4, 5, 0, 1, 2)

    def copies(k):
        return (
            pltpu.make_async_copy(near_ref.at[k], image.at[k, pl.ds(0, split)], sems.at[k, 0]),
            pltpu.make_async_copy(far_ref.at[k], image.at[k, pl.ds(split, 2048 - split)], sems.at[k, 1]),
            pltpu.make_async_copy(conduction_ref.at[:, k], right.at[k], sems.at[k, 2]),
        )

    for k in order:
        for copy in copies(k):
            copy.start()
    places = []
    for step in B_STEPS:
        b_now = lax.rem(along_b + (step + 4), 4)
        for block in range(8):
            a_now = lax.rem(along_a + (A_STEPS[block] + 4), 4)
            z_now = lax.rem(z_lo + Z_STEPS[block], 2)
            x_now = jnp.where(core == 0, a_now, b_now)
            y_now = jnp.where(core == 0, b_now, a_now)
            places.append(y_now * 8 + z_now * 4 + x_now)
    lane = lax.broadcasted_iota(jnp.int32, (64, 128), 1)
    for k in order:
        for copy in copies(k):
            copy.wait()
        gathered = jnp.concatenate([right[k, place] for place in places], axis=0)
        full = lax.dot_general(
            image[k], gathered, (((0,), (0,)), ((), ())), preferred_element_type=jnp.float32
        )
        turned = pltpu.roll(full[64:], 64, 1)
        block = jnp.where(lane < 64, turned + full[:64], turned - full[:64])
        for row_step, lane_step in ((1, 8), (2, 16), (4, 32), (1, 64)):
            block = traded(block, row_step, lane_step)
        if k < 3:
            mine_ref[k] = block
        else:
            theirs_ref[k - 3] = block


def direct_of(pos, images, conduction):
    vmem = pl.BlockSpec(memory_space=pltpu.VMEM)
    shape = jax.ShapeDtypeStruct((3, 64, 128), jnp.float32)
    return pl.pallas_call(
        direct_kernel,
        out_shape=(shape, shape),
        in_specs=[pl.BlockSpec(memory_space=pltpu.SMEM)] + [pl.BlockSpec(memory_space=pl.ANY)] * 3,
        out_specs=(vmem, vmem),
        scratch_shapes=[
            pltpu.VMEM((6, 2048, 128), jnp.bfloat16),
            pltpu.VMEM((6, 32, 64, 128), jnp.bfloat16),
            pltpu.SemaphoreType.DMA((6, 3)),
        ],
        compiler_params=pltpu.CompilerParams(vmem_limit_bytes=60 * 1024 * 1024),
        cost_estimate=pl.CostEstimate(
            flops=2 * 6 * 2048 * 128 * 128, bytes_accessed=7 * 1024 * 1024, transcendentals=0
        ),
    )(pos, *images, conduction)


def exchange_kernel(first_ref, second_ref, third_ref, fourth_ref, out_ref):
    for offset in range(NOFF):
        for k in range(3):
            total = (first_ref[offset, k] + second_ref[offset, k]) + (
                third_ref[offset, k] + fourth_ref[offset, k]
            )
            out_ref[offset, k] = traded(2.0 * total, 1, 64)


def exchange_of(pieces):
    vmem = pl.BlockSpec(memory_space=pltpu.VMEM)
    return pl.pallas_call(
        exchange_kernel,
        out_shape=jax.ShapeDtypeStruct((NOFF, 3, 64, 128), jnp.float32),
        in_specs=[vmem] * 4,
        out_specs=vmem,
    )(*pieces)


def three_pieces(values):
    high = lax.reduce_precision(values, 8, 7)
    rest = values - high
    middle = lax.reduce_precision(rest, 8, 7)
    low = rest - middle
    return jnp.stack([high, middle, low], axis=-1).astype(jnp.bfloat16)


def exchange_spread(pair_vc, coulomb):
    main = pair_vc.reshape(KX_DEV, 8, 3, 64, 128)
    last = main[:, :, 2:]
    before = jnp.concatenate([last[:, 7:], last[:, :7]], axis=1)
    sent = jnp.concatenate([before, main], axis=2)
    sent = jnp.transpose(sent, (1, 0, 2, 3, 4)).reshape(8, 16, 64, 128)
    extra = jnp.pad(three_pieces(coulomb), ((0, 0), (0, 125)))
    return jnp.concatenate([sent, jnp.broadcast_to(extra, (8, 1, 64, 128))], axis=1)


def exchange_sums(here, ahead, near_coulomb, offsets, y):
    left = here[:, :, 1:].astype(jnp.float32)
    scaled = (near_coulomb.reshape(8, 1, 1, 64, 1) * left).astype(jnp.bfloat16)
    special = jnp.where(offsets[0, 1] == NKY - 1, 0, 1)
    plain_x = offsets[1 - special, 0]
    shifted = ahead[:, :, :3]
    joined = jnp.concatenate([here[:, :, 1:], ahead[:, :, 1:]], axis=1)
    plain = lax.dynamic_slice_in_dim(joined, plain_x, KX_DEV, 1)

    def products(right):
        full = jnp.einsum("sabgp,sabgq->abpq", scaled, right, preferred_element_type=jnp.float32)
        half = full.shape[-1] // 2
        real_part = full[..., :half, :half] + full[..., half:, half:]
        imag_part = full[..., :half, half:] - full[..., half:, :half]
        return jnp.concatenate([real_part, imag_part], axis=-1)

    of_special = products(shifted)
    of_plain = products(plain)
    terms = jnp.stack(
        [jnp.where(special == 0, of_special, of_plain), jnp.where(special == 0, of_plain, of_special)],
        axis=1,
    )
    pieces = [lax.dynamic_index_in_dim(terms, y, 0, keepdims=False)]
    for step in (1, 2, 3):
        piece = lax.dynamic_index_in_dim(terms, lax.rem(y + step, 4), 0, keepdims=False)
        pieces.append(send(piece, along_y(step)))
    return pieces


def both_cores(dens, core):
    mine = lax.dynamic_index_in_dim(dens, core, 0, keepdims=False)
    theirs = lax.dynamic_index_in_dim(dens, 1 - core, 0, keepdims=False)
    got = send(theirs, other_core())
    return jnp.concatenate([mine.reshape(32, 3, 64, 128), got.reshape(32, 3, 64, 128)], axis=1)


def spread(packed, groups=None):
    return lax.all_to_all(
        packed, "ga", split_axis=0, concat_axis=0, tiled=True, axis_index_groups=groups
    )


def local(pair_vc, coulomb, dens_cc, dens_vv, screen, offsets):
    ka = lax.axis_index("ka")
    ga = lax.axis_index("ga")
    core = lax.rem(ka, 2)
    y, z_lo, x = ga // 8, lax.rem(ga // 4, 2), lax.rem(ga, 4)
    pos = jnp.stack([x, y, z_lo, core]).astype(jnp.int32)
    after = lax.optimization_barrier

    rows = lax.dynamic_index_in_dim(screen, core, 0, keepdims=True)
    rows = jnp.concatenate([rows, send(rows, along_z())], axis=0)
    sent = exchange_spread(pair_vc, coulomb)
    sent, rows = after((sent, rows))
    near = [send(rows, along_first(step)) for step in (1, -1)]
    across = send(rows, along_first(2))
    here = spread(sent, [[b * 8 + i for i in range(8)] for b in range(4)])
    valence = both_cores(dens_vv, core)
    valence, near, across = after((valence, near, across))
    rows = jnp.concatenate([rows, *near, across], axis=0)
    behind = send(rows, along_second(1))
    ahead = send(rows, along_second(-1))
    valence = spread(valence)

    near_coulomb = jnp.sum(here[:, 16, :, :3].astype(jnp.float32), axis=-1)
    here = here[:, :16].reshape(8, KX_DEV, 4, 64, 128)
    next_rows = send(here, ka_back())

    conduction = both_cores(dens_cc, core)
    conduction, valence = after((conduction, valence))
    next_rows, behind, ahead = after((next_rows, behind, ahead))
    far_low, far_high = send(behind[:4], along_second(1)), send(ahead[4:], along_second(-1))
    conduction = spread(conduction)

    valence = jnp.transpose(valence, (0, 2, 1, 3)).reshape(2048, 768)
    images = [image_of((rows, behind, ahead), valence), image_of((far_low, far_high), valence)]
    exch = exchange_sums(here, next_rows, near_coulomb, offsets, y)

    theirs, mine = direct_of(pos, images, conduction)
    theirs = send(theirs, other_core())
    direct = jnp.where((jnp.arange(NOFF) == core)[:, None, None, None], mine[None], theirs[None])
    out = (exchange_of(exch) - direct).reshape(NOFF, 3, 32, 2, 128)
    return jnp.transpose(out, (0, 3, 1, 2, 4)).reshape(NOFF, 2, 3, 4096)


def solution(mesh):
    placed = (
        P("ka", "ga", None),
        P("ga"),
        P(None, "ka", "ga", None),
        P(None, "ka", "ga", None),
        P(None, "ga", None),
        P(),
    )
    return jax.shard_map(
        local,
        mesh=mesh,
        in_specs=placed,
        out_specs=P(None, None, ("ka", "ga"), None),
        check_vma=False,
    )
```

```python
import functools

import jax
import jax.numpy as jnp
from jax import lax
from jax.experimental import pallas as pl
from jax.experimental.pallas import tpu as pltpu
from jax.sharding import PartitionSpec as P

NV = 8
NC = 8
NKY = 24
KX_DEV = 4
NOFF = 2
AXES = ("ka", "ga")
A_STEPS = (0, 0, -1, -1, 1, 1, 2, 2)
Z_STEPS = (0, 1, 0, 1, 0, 1, 0, 1)
B_STEPS = (0, -1, 1, 2)


def index_of(x, y, z_hi, z_lo, core):
    return (z_hi * 2 + core) * 32 + (y % 4) * 8 + (z_lo % 2) * 4 + x % 4


def route(move):
    pairs = []
    for source in range(128):
        ka, ga = divmod(source, 32)
        z_hi, core = divmod(ka, 2)
        y, rest = divmod(ga, 8)
        z_lo, x = divmod(rest, 4)
        pairs.append((source, move(x, y, z_hi, z_lo, core)))
    return pairs


def along_first(step):
    return route(
        lambda x, y, h, l, c: index_of(x + step, y, h, l, c) if c == 0 else index_of(x, y + step, h, l, c)
    )


def along_second(step):
    return route(
        lambda x, y, h, l, c: index_of(x, y + step, h, l, c) if c == 0 else index_of(x + step, y, h, l, c)
    )


def along_y(step):
    return route(lambda x, y, h, l, c: index_of(x, y + step, h, l, c))


def along_z():
    return route(lambda x, y, h, l, c: index_of(x, y, h, l + 1, c))


def other_core():
    return route(lambda x, y, h, l, c: index_of(x, y, h, l, 1 - c))


def ka_back():
    return [(i, (i - 32) % 128) for i in range(128)]


def ka_back_j_ahead():
    pairs = []
    for source in range(128):
        ka, ga = divmod(source, 32)
        y, j = divmod(ga, 8)
        pairs.append((source, ((ka - 1) % 4) * 32 + y * 8 + (j + 1) % 8))
    return pairs


def send(array, pairs):
    return lax.ppermute(array, AXES, pairs)


def image_kernel(*refs):
    valence_ref, out_ref = refs[-2], refs[-1]
    first = 0
    for rows_ref in refs[:-2]:
        blocks, depth, width = rows_ref.shape
        for block in range(0, blocks, 4):
            rows = rows_ref[block : block + 4].reshape(4 * depth, width)
            image = jnp.dot(rows, valence_ref[...], preferred_element_type=jnp.float32).astype(jnp.bfloat16)
            for k in range(6):
                out_ref[k, first : first + 4 * depth] = image[:, k * 128 : (k + 1) * 128]
            first += 4 * depth


def image_of(parts, valence):
    vmem = pl.BlockSpec(memory_space=pltpu.VMEM)
    count = sum(part.shape[0] * part.shape[1] for part in parts)
    return pl.pallas_call(
        image_kernel,
        out_shape=jax.ShapeDtypeStruct((6, count, 128), jnp.bfloat16),
        in_specs=[vmem] * (len(parts) + 1),
        out_specs=vmem,
        compiler_params=pltpu.CompilerParams(vmem_limit_bytes=18 * 1024 * 1024),
        cost_estimate=pl.CostEstimate(
            flops=2 * count * valence.shape[0] * valence.shape[1],
            bytes_accessed=2 * (count * 2048 + valence.size + count * valence.shape[1]),
            transcendentals=0,
        ),
    )(*parts, valence)


def traded(block, row_step, lane_step):
    row_bit = (lax.broadcasted_iota(jnp.int32, (64, 128), 0) & row_step) != 0
    lane_bit = (lax.broadcasted_iota(jnp.int32, (64, 128), 1) & lane_step) != 0
    up = pltpu.roll(pltpu.roll(block, 64 - row_step, 0), lane_step, 1)
    down = pltpu.roll(pltpu.roll(block, row_step, 0), 128 - lane_step, 1)
    return jnp.where(row_bit == lane_bit, block, jnp.where(row_bit, down, up))


def direct_kernel(pos_ref, near_ref, far_ref, conduction_ref, theirs_ref, mine_ref, image, right, sems):
    x, y, z_lo, core = pos_ref[0], pos_ref[1], pos_ref[2], pos_ref[3]
    along_a = jnp.where(core == 0, x, y)
    along_b = jnp.where(core == 0, y, x)
    split = near_ref.shape[1]
    order = (3, 4, 5, 0, 1, 2)

    def copies(k):
        return (
            pltpu.make_async_copy(near_ref.at[k], image.at[k, pl.ds(0, split)], sems.at[k, 0]),
            pltpu.make_async_copy(far_ref.at[k], image.at[k, pl.ds(split, 2048 - split)], sems.at[k, 1]),
            pltpu.make_async_copy(conduction_ref.at[:, k], right.at[k], sems.at[k, 2]),
        )

    for k in order:
        for copy in copies(k):
            copy.start()
    places = []
    for step in B_STEPS:
        b_now = lax.rem(along_b + (step + 4), 4)
        for block in range(8):
            a_now = lax.rem(along_a + (A_STEPS[block] + 4), 4)
            z_now = lax.rem(z_lo + Z_STEPS[block], 2)
            x_now = jnp.where(core == 0, a_now, b_now)
            y_now = jnp.where(core == 0, b_now, a_now)
            places.append(y_now * 8 + z_now * 4 + x_now)
    lane = lax.broadcasted_iota(jnp.int32, (64, 128), 1)
    for position, k in enumerate(order):
        if position % 3 == 0:
            for later in order[position : position + 3]:
                for copy in copies(later):
                    copy.wait()
        gathered = jnp.concatenate([right[k, place] for place in places], axis=0)
        full = lax.dot_general(
            image[k], gathered, (((0,), (0,)), ((), ())), preferred_element_type=jnp.float32
        )
        turned = pltpu.roll(full[64:], 64, 1)
        block = jnp.where(lane < 64, turned + full[:64], turned - full[:64])
        for row_step, lane_step in ((1, 8), (2, 16), (4, 32), (1, 64)):
            block = traded(block, row_step, lane_step)
        if k < 3:
            mine_ref[k] = block
        else:
            theirs_ref[k - 3] = block


def direct_of(pos, images, conduction):
    vmem = pl.BlockSpec(memory_space=pltpu.VMEM)
    shape = jax.ShapeDtypeStruct((3, 64, 128), jnp.float32)
    return pl.pallas_call(
        direct_kernel,
        out_shape=(shape, shape),
        in_specs=[pl.BlockSpec(memory_space=pltpu.SMEM)] + [pl.BlockSpec(memory_space=pl.ANY)] * 3,
        out_specs=(vmem, vmem),
        scratch_shapes=[
            pltpu.VMEM((6, 2048, 128), jnp.bfloat16),
            pltpu.VMEM((6, 32, 64, 128), jnp.bfloat16),
            pltpu.SemaphoreType.DMA((6, 3)),
        ],
        compiler_params=pltpu.CompilerParams(vmem_limit_bytes=60 * 1024 * 1024),
        cost_estimate=pl.CostEstimate(
            flops=2 * 6 * 2048 * 128 * 128, bytes_accessed=7 * 1024 * 1024, transcendentals=0
        ),
    )(pos, *images, conduction)


def exchange_kernel(first_ref, second_ref, third_ref, fourth_ref, out_ref):
    for offset in range(NOFF):
        for k in range(3):
            total = (first_ref[offset, k] + second_ref[offset, k]) + (
                third_ref[offset, k] + fourth_ref[offset, k]
            )
            out_ref[offset, k] = traded(2.0 * total, 1, 64)


def exchange_of(pieces):
    vmem = pl.BlockSpec(memory_space=pltpu.VMEM)
    return pl.pallas_call(
        exchange_kernel,
        out_shape=jax.ShapeDtypeStruct((NOFF, 3, 64, 128), jnp.float32),
        in_specs=[vmem] * 4,
        out_specs=vmem,
    )(*pieces)


def three_pieces(values):
    high = lax.reduce_precision(values, 8, 7)
    rest = values - high
    middle = lax.reduce_precision(rest, 8, 7)
    low = rest - middle
    return jnp.stack([high, middle, low], axis=-1).astype(jnp.bfloat16)


def exchange_spread(pair_vc, coulomb):
    main = pair_vc.reshape(KX_DEV, 8, 3, 64, 128)
    last = main[:, :, 2:]
    before = jnp.concatenate([last[:, 7:], last[:, :7]], axis=1)
    sent = jnp.concatenate([before, main], axis=2)
    sent = jnp.transpose(sent, (1, 0, 2, 3, 4)).reshape(8, 16, 64, 128)
    extra = jnp.pad(three_pieces(coulomb), ((0, 0), (0, 125)))
    return jnp.concatenate([sent, jnp.broadcast_to(extra, (8, 1, 64, 128))], axis=1)


def exchange_sums(here, ahead, near_coulomb, offsets, y):
    left = here[:, :, 1:].astype(jnp.float32)
    scaled = (near_coulomb.reshape(8, 1, 1, 64, 1) * left).astype(jnp.bfloat16)
    special = jnp.where(offsets[0, 1] == NKY - 1, 0, 1)
    plain_x = offsets[1 - special, 0]
    shifted = ahead[:, :, :3]
    joined = jnp.concatenate([here[:, :, 1:], ahead[:, :, 1:]], axis=1)
    plain = lax.dynamic_slice_in_dim(joined, plain_x, KX_DEV, 1)

    def products(right):
        full = jnp.einsum("sabgp,sabgq->abpq", scaled, right, preferred_element_type=jnp.float32)
        half = full.shape[-1] // 2
        real_part = full[..., :half, :half] + full[..., half:, half:]
        imag_part = full[..., :half, half:] - full[..., half:, :half]
        return jnp.concatenate([real_part, imag_part], axis=-1)

    of_special = products(shifted)
    of_plain = products(plain)
    terms = jnp.stack(
        [jnp.where(special == 0, of_special, of_plain), jnp.where(special == 0, of_plain, of_special)],
        axis=1,
    )
    pieces = [lax.dynamic_index_in_dim(terms, y, 0, keepdims=False)]
    for step in (1, 2, 3):
        piece = lax.dynamic_index_in_dim(terms, lax.rem(y + step, 4), 0, keepdims=False)
        pieces.append(send(piece, along_y(step)))
    return pieces


def both_cores(dens, core):
    mine = lax.dynamic_index_in_dim(dens, core, 0, keepdims=False)
    theirs = lax.dynamic_index_in_dim(dens, 1 - core, 0, keepdims=False)
    got = send(theirs, other_core())
    return jnp.concatenate([mine.reshape(32, 3, 64, 128), got.reshape(32, 3, 64, 128)], axis=1)


def spread(packed, groups=None):
    return lax.all_to_all(
        packed, "ga", split_axis=0, concat_axis=0, tiled=True, axis_index_groups=groups
    )


def local(pair_vc, coulomb, dens_cc, dens_vv, screen, offsets):
    ka = lax.axis_index("ka")
    ga = lax.axis_index("ga")
    core = lax.rem(ka, 2)
    y, z_lo, x = ga // 8, lax.rem(ga // 4, 2), lax.rem(ga, 4)
    pos = jnp.stack([x, y, z_lo, core]).astype(jnp.int32)
    after = lax.optimization_barrier

    rows = lax.dynamic_index_in_dim(screen, core, 0, keepdims=True)
    rows = jnp.concatenate([rows, send(rows, along_z())], axis=0)
    sent = exchange_spread(pair_vc, coulomb)
    sent, rows = after((sent, rows))
    near = [send(rows, along_first(step)) for step in (1, -1)]
    across = send(rows, along_first(2))
    here = spread(sent, [[b * 8 + i for i in range(8)] for b in range(4)])
    valence = both_cores(dens_vv, core)
    valence, near, across = after((valence, near, across))
    rows = jnp.concatenate([rows, *near, across], axis=0)
    behind = send(rows, along_second(1))
    ahead = send(rows, along_second(-1))
    valence = spread(valence)

    near_coulomb = jnp.sum(here[:, 16, :, :3].astype(jnp.float32), axis=-1)
    here = here[:, :16].reshape(8, KX_DEV, 4, 64, 128)
    next_rows = send(here, ka_back())

    conduction = both_cores(dens_cc, core)
    conduction, valence = after((conduction, valence))
    next_rows, behind, ahead = after((next_rows, behind, ahead))
    far_low, far_high = send(behind[:4], along_second(1)), send(ahead[4:], along_second(-1))
    conduction = spread(conduction)

    valence = jnp.transpose(valence, (0, 2, 1, 3)).reshape(2048, 768)
    images = [image_of((rows, behind, ahead), valence), image_of((far_low, far_high), valence)]
    exch = exchange_sums(here, next_rows, near_coulomb, offsets, y)

    theirs, mine = direct_of(pos, images, conduction)
    theirs = send(theirs, other_core())
    direct = jnp.where((jnp.arange(NOFF) == core)[:, None, None, None], mine[None], theirs[None])
    out = (exchange_of(exch) - direct).reshape(NOFF, 3, 32, 2, 128)
    return jnp.transpose(out, (0, 3, 1, 2, 4)).reshape(NOFF, 2, 3, 4096)


def solution(mesh):
    placed = (
        P("ka", "ga", None),
        P("ga"),
        P(None, "ka", "ga", None),
        P(None, "ka", "ga", None),
        P(None, "ga", None),
        P(),
    )
    return jax.shard_map(
        local,
        mesh=mesh,
        in_specs=placed,
        out_specs=P(None, None, ("ka", "ga"), None),
        check_vma=False,
    )
```

```python
import functools

import jax
import jax.numpy as jnp
from jax import lax
from jax.experimental import pallas as pl
from jax.experimental.pallas import tpu as pltpu
from jax.sharding import PartitionSpec as P

NV = 8
NC = 8
NKY = 24
KX_DEV = 4
NOFF = 2
AXES = ("ka", "ga")
A_STEPS = (0, 0, -1, -1, 1, 1, 2, 2)
Z_STEPS = (0, 1, 0, 1, 0, 1, 0, 1)
B_STEPS = (0, -1, 1, 2)


def index_of(x, y, z_hi, z_lo, core):
    return (z_hi * 2 + core) * 32 + (y % 4) * 8 + (z_lo % 2) * 4 + x % 4


def route(move):
    pairs = []
    for source in range(128):
        ka, ga = divmod(source, 32)
        z_hi, core = divmod(ka, 2)
        y, rest = divmod(ga, 8)
        z_lo, x = divmod(rest, 4)
        pairs.append((source, move(x, y, z_hi, z_lo, core)))
    return pairs


def along_first(step):
    return route(
        lambda x, y, h, l, c: index_of(x + step, y, h, l, c) if c == 0 else index_of(x, y + step, h, l, c)
    )


def along_second(step):
    return route(
        lambda x, y, h, l, c: index_of(x, y + step, h, l, c) if c == 0 else index_of(x + step, y, h, l, c)
    )


def along_y(step):
    return route(lambda x, y, h, l, c: index_of(x, y + step, h, l, c))


def along_z():
    return route(lambda x, y, h, l, c: index_of(x, y, h, l + 1, c))


def other_core():
    return route(lambda x, y, h, l, c: index_of(x, y, h, l, 1 - c))


def ka_back():
    return [(i, (i - 32) % 128) for i in range(128)]


def ka_back_j_ahead():
    pairs = []
    for source in range(128):
        ka, ga = divmod(source, 32)
        y, j = divmod(ga, 8)
        pairs.append((source, ((ka - 1) % 4) * 32 + y * 8 + (j + 1) % 8))
    return pairs


def send(array, pairs):
    return lax.ppermute(array, AXES, pairs)


def image_kernel(*refs):
    valence_ref, out_ref = refs[-2], refs[-1]
    first = 0
    for rows_ref in refs[:-2]:
        blocks, depth, width = rows_ref.shape
        for block in range(0, blocks, 4):
            rows = rows_ref[block : block + 4].reshape(4 * depth, width)
            image = jnp.dot(rows, valence_ref[...], preferred_element_type=jnp.float32).astype(jnp.bfloat16)
            for k in range(6):
                out_ref[k, first : first + 4 * depth] = image[:, k * 128 : (k + 1) * 128]
            first += 4 * depth


def image_of(parts, valence):
    vmem = pl.BlockSpec(memory_space=pltpu.VMEM)
    count = sum(part.shape[0] * part.shape[1] for part in parts)
    return pl.pallas_call(
        image_kernel,
        out_shape=jax.ShapeDtypeStruct((6, count, 128), jnp.bfloat16),
        in_specs=[vmem] * (len(parts) + 1),
        out_specs=vmem,
        compiler_params=pltpu.CompilerParams(vmem_limit_bytes=18 * 1024 * 1024),
        cost_estimate=pl.CostEstimate(
            flops=2 * count * valence.shape[0] * valence.shape[1],
            bytes_accessed=2 * (count * 2048 + valence.size + count * valence.shape[1]),
            transcendentals=0,
        ),
    )(*parts, valence)


def traded(block, row_step, lane_step):
    row_bit = (lax.broadcasted_iota(jnp.int32, (64, 128), 0) & row_step) != 0
    lane_bit = (lax.broadcasted_iota(jnp.int32, (64, 128), 1) & lane_step) != 0
    up = pltpu.roll(pltpu.roll(block, 64 - row_step, 0), lane_step, 1)
    down = pltpu.roll(pltpu.roll(block, row_step, 0), 128 - lane_step, 1)
    return jnp.where(row_bit == lane_bit, block, jnp.where(row_bit, down, up))


def direct_kernel(pos_ref, near_ref, far_ref, conduction_ref, theirs_ref, mine_ref, image, right, sems):
    x, y, z_lo, core = pos_ref[0], pos_ref[1], pos_ref[2], pos_ref[3]
    along_a = jnp.where(core == 0, x, y)
    along_b = jnp.where(core == 0, y, x)
    split = near_ref.shape[1]
    order = (3, 4, 5, 0, 1, 2)

    def copies(k):
        return (
            pltpu.make_async_copy(near_ref.at[k], image.at[k, pl.ds(0, split)], sems.at[k, 0]),
            pltpu.make_async_copy(far_ref.at[k], image.at[k, pl.ds(split, 2048 - split)], sems.at[k, 1]),
            pltpu.make_async_copy(conduction_ref.at[:, k], right.at[k], sems.at[k, 2]),
        )

    for k in order:
        for copy in copies(k):
            copy.start()
    places = []
    for step in B_STEPS:
        b_now = lax.rem(along_b + (step + 4), 4)
        for block in range(8):
            a_now = lax.rem(along_a + (A_STEPS[block] + 4), 4)
            z_now = lax.rem(z_lo + Z_STEPS[block], 2)
            x_now = jnp.where(core == 0, a_now, b_now)
            y_now = jnp.where(core == 0, b_now, a_now)
            places.append(y_now * 8 + z_now * 4 + x_now)
    lane = lax.broadcasted_iota(jnp.int32, (64, 128), 1)
    for position, k in enumerate(order):
        if position % 3 == 0:
            for later in order[position : position + 3]:
                for copy in copies(later):
                    copy.wait()
        gathered = jnp.concatenate([right[k, place] for place in places], axis=0)
        full = lax.dot_general(
            image[k], gathered, (((0,), (0,)), ((), ())), preferred_element_type=jnp.float32
        )
        turned = pltpu.roll(full[64:], 64, 1)
        block = jnp.where(lane < 64, turned + full[:64], turned - full[:64])
        for row_step, lane_step in ((1, 8), (2, 16), (4, 32), (1, 64)):
            block = traded(block, row_step, lane_step)
        if k < 3:
            mine_ref[k] = block
        else:
            theirs_ref[k - 3] = block


def direct_of(pos, images, conduction):
    vmem = pl.BlockSpec(memory_space=pltpu.VMEM)
    shape = jax.ShapeDtypeStruct((3, 64, 128), jnp.float32)
    return pl.pallas_call(
        direct_kernel,
        out_shape=(shape, shape),
        in_specs=[pl.BlockSpec(memory_space=pltpu.SMEM)] + [pl.BlockSpec(memory_space=pl.ANY)] * 3,
        out_specs=(vmem, vmem),
        scratch_shapes=[
            pltpu.VMEM((6, 2048, 128), jnp.bfloat16),
            pltpu.VMEM((6, 32, 64, 128), jnp.bfloat16),
            pltpu.SemaphoreType.DMA((6, 3)),
        ],
        compiler_params=pltpu.CompilerParams(vmem_limit_bytes=60 * 1024 * 1024),
        cost_estimate=pl.CostEstimate(
            flops=2 * 6 * 2048 * 128 * 128, bytes_accessed=7 * 1024 * 1024, transcendentals=0
        ),
    )(pos, *images, conduction)


def exchange_kernel(first_ref, second_ref, third_ref, fourth_ref, out_ref):
    for offset in range(NOFF):
        for k in range(3):
            total = (first_ref[offset, k] + second_ref[offset, k]) + (
                third_ref[offset, k] + fourth_ref[offset, k]
            )
            out_ref[offset, k] = traded(2.0 * total, 1, 64)


def exchange_of(pieces):
    vmem = pl.BlockSpec(memory_space=pltpu.VMEM)
    return pl.pallas_call(
        exchange_kernel,
        out_shape=jax.ShapeDtypeStruct((NOFF, 3, 64, 128), jnp.float32),
        in_specs=[vmem] * 4,
        out_specs=vmem,
    )(*pieces)


def three_pieces(values):
    high = lax.reduce_precision(values, 8, 7)
    rest = values - high
    middle = lax.reduce_precision(rest, 8, 7)
    low = rest - middle
    return jnp.stack([high, middle, low], axis=-1).astype(jnp.bfloat16)


def exchange_spread(pair_vc, coulomb):
    main = pair_vc.reshape(KX_DEV, 8, 3, 64, 128)
    last = main[:, :, 2:]
    before = jnp.concatenate([last[:, 7:], last[:, :7]], axis=1)
    sent = jnp.concatenate([before, main], axis=2)
    sent = jnp.transpose(sent, (1, 0, 2, 3, 4)).reshape(8, 16, 64, 128)
    extra = jnp.pad(three_pieces(coulomb), ((0, 0), (0, 125)))
    return jnp.concatenate([sent, jnp.broadcast_to(extra, (8, 1, 64, 128))], axis=1)


def exchange_sums(here, ahead, near_coulomb, offsets, y):
    left = here[:, :, 1:].astype(jnp.float32)
    scaled = (near_coulomb.reshape(8, 1, 1, 64, 1) * left).astype(jnp.bfloat16)
    special = jnp.where(offsets[0, 1] == NKY - 1, 0, 1)
    plain_x = offsets[1 - special, 0]
    shifted = ahead[:, :, :3]
    joined = jnp.concatenate([here[:, :, 1:], ahead[:, :, 1:]], axis=1)
    plain = lax.dynamic_slice_in_dim(joined, plain_x, KX_DEV, 1)

    def products(right):
        full = jnp.einsum("sabgp,sabgq->abpq", scaled, right, preferred_element_type=jnp.float32)
        half = full.shape[-1] // 2
        real_part = full[..., :half, :half] + full[..., half:, half:]
        imag_part = full[..., :half, half:] - full[..., half:, :half]
        return jnp.concatenate([real_part, imag_part], axis=-1)

    of_special = products(shifted)
    of_plain = products(plain)
    terms = jnp.stack(
        [jnp.where(special == 0, of_special, of_plain), jnp.where(special == 0, of_plain, of_special)],
        axis=1,
    )
    pieces = [lax.dynamic_index_in_dim(terms, y, 0, keepdims=False)]
    for step in (1, 2, 3):
        piece = lax.dynamic_index_in_dim(terms, lax.rem(y + step, 4), 0, keepdims=False)
        pieces.append(send(piece, along_y(step)))
    return pieces


def both_cores(dens, core):
    mine = lax.dynamic_index_in_dim(dens, core, 0, keepdims=False)
    theirs = lax.dynamic_index_in_dim(dens, 1 - core, 0, keepdims=False)
    got = send(theirs, other_core())
    return jnp.concatenate([mine.reshape(32, 3, 64, 128), got.reshape(32, 3, 64, 128)], axis=1)


def spread(packed, groups=None):
    return lax.all_to_all(
        packed, "ga", split_axis=0, concat_axis=0, tiled=True, axis_index_groups=groups
    )


def local(pair_vc, coulomb, dens_cc, dens_vv, screen, offsets):
    ka = lax.axis_index("ka")
    ga = lax.axis_index("ga")
    core = lax.rem(ka, 2)
    y, z_lo, x = ga // 8, lax.rem(ga // 4, 2), lax.rem(ga, 4)
    pos = jnp.stack([x, y, z_lo, core]).astype(jnp.int32)
    after = lax.optimization_barrier

    rows = lax.dynamic_index_in_dim(screen, core, 0, keepdims=True)
    rows = jnp.concatenate([rows, send(rows, along_z())], axis=0)
    sent = exchange_spread(pair_vc, coulomb)
    sent, rows = after((sent, rows))
    near = [send(rows, along_first(step)) for step in (1, -1)]
    across = send(rows, along_first(2))
    here = spread(sent, [[b * 8 + i for i in range(8)] for b in range(4)])
    valence = both_cores(dens_vv, core)
    valence, near, across = after((valence, near, across))
    rows = jnp.concatenate([rows, *near, across], axis=0)
    behind = send(rows, along_second(1))
    ahead = send(rows, along_second(-1))
    valence = spread(valence)

    near_coulomb = jnp.sum(here[:, 16, :, :3].astype(jnp.float32), axis=-1)
    here = here[:, :16].reshape(8, KX_DEV, 4, 64, 128)
    next_rows = send(here, ka_back())

    conduction = both_cores(dens_cc, core)
    conduction, valence = after((conduction, valence))
    far_low, far_high = send(behind[:4], along_second(1)), send(ahead[4:], along_second(-1))
    next_rows, behind, ahead = after((next_rows, behind, ahead))
    conduction = spread(conduction)

    valence = jnp.transpose(valence, (0, 2, 1, 3)).reshape(2048, 768)
    images = [image_of((rows, behind, ahead), valence), image_of((far_low, far_high), valence)]
    exch = exchange_sums(here, next_rows, near_coulomb, offsets, y)

    theirs, mine = direct_of(pos, images, conduction)
    theirs = send(theirs, other_core())
    direct = jnp.where((jnp.arange(NOFF) == core)[:, None, None, None], mine[None], theirs[None])
    out = (exchange_of(exch) - direct).reshape(NOFF, 3, 32, 2, 128)
    return jnp.transpose(out, (0, 3, 1, 2, 4)).reshape(NOFF, 2, 3, 4096)


def solution(mesh):
    placed = (
        P("ka", "ga", None),
        P("ga"),
        P(None, "ka", "ga", None),
        P(None, "ka", "ga", None),
        P(None, "ga", None),
        P(),
    )
    return jax.shard_map(
        local,
        mesh=mesh,
        in_specs=placed,
        out_specs=P(None, None, ("ka", "ga"), None),
        check_vma=False,
    )
```
